32 devices in a mesh: shard: 4 (over z), ctx: 2 (over x), tp: 4 (over y, core).
Axes of the slice: x: 2, y: 2, z: 4, core: 2. Of those that a mesh axis runs over, the one named last changes fastest.
Arguments:
- inputs: float32 [4, 4096, 1536], P('shard', 'ctx'), may hold values from -6 to 6
- lengths: int32 [4], P('shard'), may hold values from 1024 to 4096, as said below
- rec_proj: float32 [1536, 2048], P(('shard', 'ctx'), 'tp'), may hold values from -0.15625 to 0.15625
- gate_proj: float32 [1536, 2048], P(('shard', 'ctx'), 'tp'), may hold values from -0.15625 to 0.15625
- out_proj: float32 [1536, 2048], P(('shard', 'ctx'), 'tp'), may hold values from -0.125 to 0.125
- ffn_gate: float32 [1536, 4608], P(('shard', 'ctx'), 'tp'), may hold values from -0.15625 to 0.15625
- ffn_up: float32 [1536, 4608], P(('shard', 'ctx'), 'tp'), may hold values from -0.15625 to 0.15625
- ffn_down: float32 [1536, 4608], P(('shard', 'ctx'), 'tp'), may hold values from -0.09375 to 0.09375
- conv_weight: float32 [4, 2048], P(None, 'tp'), may hold values from -3 to 3
- conv_bias: float32 [2048], P('tp'), may hold values from -3 to 3
- a_gate: float32 [16, 128, 128], P('tp'), may hold values from -0.5 to 0.5
- i_gate: float32 [16, 128, 128], P('tp'), may hold values from -0.5 to 0.5
- a_bias: float32 [2048], P('tp'), may hold values from -4 to 4
- i_bias: float32 [2048], P('tp'), may hold values from -4 to 4
- lambda_param: float32 [2048], P('tp'), may hold values from 3 to 8
- rec_norm: float32 [1536], replicated, may hold values from 0.1 to 1.9
- ffn_norm: float32 [1536], replicated, may hold values from 0.1 to 1.9
- cotangent: float32 [4, 4096, 1536], P('shard', 'ctx'), may hold values from -6 to 6
Outputs:
- block_out: float32 [4, 4096, 1536], P('shard', 'ctx')
- input_grad: float32 [4, 4096, 1536], P('shard', 'ctx')
- grad_rec_proj: float32 [1536, 2048], P(('shard', 'ctx'), 'tp')
- grad_gate_proj: float32 [1536, 2048], P(('shard', 'ctx'), 'tp')
- grad_out_proj: float32 [1536, 2048], P(('shard', 'ctx'), 'tp')
- grad_ffn_gate: float32 [1536, 4608], P(('shard', 'ctx'), 'tp')
- grad_ffn_up: float32 [1536, 4608], P(('shard', 'ctx'), 'tp')
- grad_ffn_down: float32 [1536, 4608], P(('shard', 'ctx'), 'tp')
- grad_conv_weight: float32 [4, 2048], P(None, 'tp')
- grad_conv_bias: float32 [2048], P('tp')
- grad_a_gate: float32 [16, 128, 128], P('tp')
- grad_i_gate: float32 [16, 128, 128], P('tp')
- grad_a_bias: float32 [2048], P('tp')
- grad_i_bias: float32 [2048], P('tp')
- grad_lambda: float32 [2048], P('tp')
- grad_rec_norm: float32 [1536], replicated
- grad_ffn_norm: float32 [1536], replicated
The draws below stay inside these ranges and needn't reach their ends.
Inputs may be any that keep to these rules, and one draw needn't show every extreme that they name: `lengths`: in each aligned group of 1 sequence, one drawn from the seed has length 4096.
All inputs are finite; a program needn't handle non-finite values.
Results may differ from the reference program's by a relative error of at most 0.0003.
Values sent between devices are 32-bit elements; how exact they have to be, the bound alone decides.
No kernel may reach another device: no remote copies, remote signals or barrier semaphores. Data moves between devices by JAX's collectives and lax.ppermute only.
A program may use at most 320 MiB of HBM per device.

```python
import jax
import jax.numpy as jnp
from jax import lax

D = 1536
H = 2048
F = 4608
NB = 16
CONV = 4
LENGTH = 4096
SEQ_DEV = 1
BW = 128
MIN_LEN = 1024
SEQS = 4


def draw_lengths(key, part):
    length_key, choose_key = jax.random.split(jax.random.fold_in(key, 17))
    group_count = SEQS // SEQ_DEV
    drawn_lengths = jax.random.randint(length_key, (SEQS,), MIN_LEN, LENGTH + 1, dtype=jnp.int32)
    chosen_slot = jax.random.randint(choose_key, (group_count,), 0, SEQ_DEV, dtype=jnp.int32)
    slot_index = jnp.arange(SEQS, dtype=jnp.int32)
    is_chosen = slot_index % SEQ_DEV == jnp.repeat(chosen_slot, SEQ_DEV)
    return jnp.where(is_chosen, LENGTH, drawn_lengths).astype(jnp.int32)


def steps_of(rng, extent, shards, low, high):
    factor_of = 1.0
    for position, parts in shards:
        steps = jax.random.uniform(jax.random.fold_in(jax.random.fold_in(rng, 6), position), (parts,), jnp.float32, low / len(shards), high / len(shards))
        factor_of = factor_of * jnp.repeat(jnp.exp(steps), extent[position] // parts).reshape((-1,) + (1,) * (len(extent) - 1 - position))
    return factor_of


def normal_values(rng, dims, deviation, limit, shards=(), held_as=jnp.bfloat16):
    drawn = deviation * jax.random.normal(rng, dims, jnp.float32)
    if shards:
        drawn = drawn * steps_of(rng, dims, shards, -0.22, 0.18)
    return jnp.clip(drawn, -limit, limit).astype(held_as)


def setup_inputs(seed: int = 0) -> dict:
    seeds = jax.random.split(jax.random.key(seed), 19)
    inputs = normal_values(seeds[0], (SEQS, LENGTH, D), 1.0, 6.0, ((0, 4), (1, 2)), jnp.float32)
    lengths = draw_lengths(jax.random.fold_in(seeds[18], 71), 0)
    rec_proj = normal_values(seeds[2], (D, H), D ** -0.5, 0.15625, ((0, 8), (1, 4)), jnp.float32)
    gate_proj = normal_values(seeds[3], (D, H), D ** -0.5, 0.15625, ((0, 8), (1, 4)), jnp.float32)
    out_proj = normal_values(seeds[4], (D, H), H ** -0.5, 0.125, ((0, 8), (1, 4)), jnp.float32)
    ffn_gate = normal_values(seeds[5], (D, F), D ** -0.5, 0.15625, ((0, 8), (1, 4)), jnp.float32)
    ffn_up = normal_values(seeds[6], (D, F), D ** -0.5, 0.15625, ((0, 8), (1, 4)), jnp.float32)
    ffn_down = normal_values(seeds[7], (D, F), F ** -0.5, 0.09375, ((0, 8), (1, 4)), jnp.float32)
    conv_weight = normal_values(seeds[8], (CONV, H), 0.5, 3.0, ((1, 4),), jnp.float32)
    conv_bias = normal_values(seeds[9], (H,), 0.5, 3.0, ((0, 4),), jnp.float32)
    a_gate = normal_values(seeds[10], (NB, BW, BW), BW ** -0.5, 0.5, ((0, 4),), jnp.float32)
    i_gate = normal_values(seeds[11], (NB, BW, BW), BW ** -0.5, 0.5, ((0, 4),), jnp.float32)
    a_bias = normal_values(seeds[12], (H,), 1.0, 4.0, ((0, 4),), jnp.float32)
    i_bias = normal_values(seeds[13], (H,), 1.0, 4.0, ((0, 4),), jnp.float32)
    lambda_param = jnp.clip(3.0 + 5.0 * jax.random.uniform(seeds[14], (H,), jnp.float32) ** steps_of(seeds[14], (H,), ((0, 4),), -0.2, 0.2), 3.0, 8.0)
    rec_norm = jnp.clip(1.0 + 0.18 * jax.random.normal(seeds[15], (D,), jnp.float32), 0.1, 1.9)
    ffn_norm = jnp.clip(1.0 + 0.18 * jax.random.normal(seeds[16], (D,), jnp.float32), 0.1, 1.9)
    cotangent = normal_values(seeds[17], (SEQS, LENGTH, D), 1.0, 6.0, ((0, 4), (1, 2)), jnp.float32)
    return {"inputs": inputs, "lengths": lengths, "rec_proj": rec_proj, "gate_proj": gate_proj, "out_proj": out_proj, "ffn_gate": ffn_gate, "ffn_up": ffn_up, "ffn_down": ffn_down, "conv_weight": conv_weight, "conv_bias": conv_bias, "a_gate": a_gate, "i_gate": i_gate, "a_bias": a_bias, "i_bias": i_bias, "lambda_param": lambda_param, "rec_norm": rec_norm, "ffn_norm": ffn_norm, "cotangent": cotangent}


HIGHEST = lax.Precision.HIGHEST
EPSILON = 1e-06
DECAY_CONST = 8.0

def affine_pair(earlier, later_pair):
    return (earlier[0] * later_pair[0], later_pair[0] * earlier[1] + later_pair[1])

def matmul(left, right):
    return jnp.dot(left, right, precision=HIGHEST, preferred_element_type=jnp.float32)

def rms_scale(values, gain):
    return values * lax.rsqrt(lax.optimization_barrier(jnp.mean(values * values, axis=-1, keepdims=True)) + EPSILON) * gain

def gelu_tanh(values):
    return jax.nn.gelu(values, approximate=True)

def forward(params, inputs, lengths):
    rec_proj, gate_proj, out_proj, ffn_gate, ffn_up, ffn_down, conv_weight, conv_bias, a_gate, i_gate, a_bias, i_bias, lambda_param, rec_norm, ffn_norm = params
    groups, length, width = inputs.shape
    row_count = groups * length
    normed_one = rms_scale(inputs, rec_norm).reshape(row_count, width)
    branch = matmul(normed_one, rec_proj).reshape(groups, length, -1)
    gate_act = gelu_tanh(matmul(normed_one, gate_proj)).reshape(groups, length, -1)
    padded_branch = jnp.pad(branch, ((0, 0), (CONV - 1, 0), (0, 0)))
    conv_out = jnp.zeros_like(branch) + conv_bias
    for offset in range(CONV):
        conv_out = conv_out + conv_weight[offset] * padded_branch[:, CONV - 1 - offset:CONV - 1 - offset + length]
    blocked = conv_out.reshape(groups, length, NB, BW)
    a_pre = jnp.einsum('gtnj,njk->gtnk', blocked, a_gate, precision=HIGHEST).reshape(groups, length, -1) + a_bias
    i_pre = jnp.einsum('gtnj,njk->gtnk', blocked, i_gate, precision=HIGHEST).reshape(groups, length, -1) + i_bias
    a_rate = jax.nn.sigmoid(a_pre)
    i_rate = jax.nn.sigmoid(i_pre)
    log_decay = -DECAY_CONST * a_rate * jax.nn.softplus(-lambda_param)
    decay_rate = jnp.exp(log_decay)
    scale_in = jnp.sqrt(-jnp.expm1(2.0 * log_decay))
    drive = scale_in * i_rate * conv_out
    cumul_decay, rec_state = lax.associative_scan(affine_pair, (decay_rate, drive), axis=1)
    mixed_rows = (rec_state * gate_act).reshape(row_count, -1)
    after_mix = inputs.reshape(row_count, width) + matmul(mixed_rows, out_proj.T)
    normed_two = rms_scale(after_mix, ffn_norm)
    hidden = gelu_tanh(matmul(normed_two, ffn_gate)) * matmul(normed_two, ffn_up)
    result = after_mix + matmul(hidden, ffn_down.T)
    valid_mask = jnp.arange(length, dtype=jnp.int32)[None, :] < lengths[:, None]
    return jnp.where(valid_mask[:, :, None], result.reshape(groups, length, width), 0.0)

def reference(inputs, lengths, rec_proj, gate_proj, out_proj, ffn_gate, ffn_up, ffn_down, conv_weight, conv_bias, a_gate, i_gate, a_bias, i_bias, lambda_param, rec_norm, ffn_norm, cotangent):
    params = (rec_proj, gate_proj, out_proj, ffn_gate, ffn_up, ffn_down, conv_weight, conv_bias, a_gate, i_gate, a_bias, i_bias, lambda_param, rec_norm, ffn_norm)
    group_size = 1
    group_count = SEQS // group_size
    block_inputs = inputs.reshape(group_count, group_size, LENGTH, D)
    block_lengths = lengths.reshape(group_count, group_size)
    block_cots = cotangent.reshape(group_count, group_size, LENGTH, D)

    def accumulate(totals, item):
        block_in, block_len, block_cot = item

        def apply_block(weights, values):
            return forward(weights, values, block_len)
        block_result, pullback = jax.vjp(apply_block, params, block_in)
        grad_params, grad_in = pullback(block_cot)
        totals = jax.tree.map(jnp.add, totals, grad_params)
        return (totals, (block_result, grad_in))
    zero_grads = jax.tree.map(jnp.zeros_like, params)
    totals, (results, grads_in) = lax.scan(accumulate, zero_grads, (block_inputs, block_lengths, block_cots))
    return (results.reshape(SEQS, LENGTH, D), grads_in.reshape(SEQS, LENGTH, D), totals[0], totals[1], totals[2], totals[3], totals[4], totals[5], totals[6], totals[7], totals[8], totals[9], totals[10], totals[11], totals[12], totals[13], totals[14])
```

```python
import functools

import jax
import jax.numpy as jnp
from jax import lax
from jax.experimental import pallas as pl
from jax.experimental.pallas import tpu as pltpu
from jax.sharding import PartitionSpec as P

HIGH = lax.Precision.HIGH
EPSILON = 1e-06
DECAY_CONST = 8.0
ROOT = 0.7978845608028654
CUBIC = 0.044715
F32 = jnp.float32
BF16 = jnp.bfloat16
VMEM_BYTES = 56 * 1024 * 1024


def matmul(left, right):
    return jnp.dot(left, right, precision=HIGH, preferred_element_type=F32)


def matmul_nt(left, right):
    return lax.dot_general(
        left, right, (((1,), (1,)), ((), ())), precision=HIGH, preferred_element_type=F32
    )


def matmul_tn(left, right):
    return lax.dot_general(
        left, right, (((0,), (0,)), ((), ())), precision=HIGH, preferred_element_type=F32
    )


def halves(values):
    high = values.astype(BF16)
    return high, (values - high.astype(F32)).astype(BF16)


def three_pass(left, right, dims):
    left_high, left_low = halves(left)
    right_high, right_low = halves(right)

    def part(one, two):
        return lax.dot_general(one, two, (dims, ((), ())), preferred_element_type=F32)

    return part(left_high, right_high) + (part(left_high, right_low) + part(left_low, right_high))


def gelu_parts(values):
    square = values * values
    curve = jnp.tanh(ROOT * values * (1.0 + CUBIC * square))
    act = 0.5 * values * (1.0 + curve)
    slope = 0.5 * (1.0 + curve) + 0.5 * values * (1.0 - curve * curve) * ROOT * (
        1.0 + 3.0 * CUBIC * square
    )
    return act, slope


def gelu(values):
    return 0.5 * values * (1.0 + jnp.tanh(ROOT * values * (1.0 + CUBIC * values * values)))


def expm1_negative(values):
    series = jnp.full_like(values, 1.0)
    for order in range(11, 1, -1):
        series = 1.0 + values * (1.0 / order) * series
    return jnp.where(values > -1.0, values * series, jnp.exp(values) - 1.0)


def decay_parts(a_rate, soft_lambda):
    log_decay = -DECAY_CONST * a_rate * soft_lambda
    return jnp.exp(log_decay), jnp.sqrt(-expm1_negative(2.0 * log_decay))


def passed_along(block, axis, distance):
    devices = range(lax.axis_size(axis))
    route = [(i - distance, i) for i in devices if i - distance in devices]
    return lax.ppermute(block, axis, route)


def rotated(block, axis, distance):
    count = lax.axis_size(axis)
    return lax.ppermute(block, axis, [(i, (i + distance) % count) for i in range(count)])


def swapped(block, axis, bit):
    return lax.ppermute(block, axis, [(i, i ^ bit) for i in range(lax.axis_size(axis))])


def carried_in(decay, state, sign):
    count = lax.axis_size("ctx")
    mine = lax.axis_index("ctx")
    place = mine if sign > 0 else count - 1 - mine
    distance = 1
    while distance < count - 1:
        earlier_decay = passed_along(decay, "ctx", sign * distance)
        earlier_state = passed_along(state, "ctx", sign * distance)
        has = place >= distance
        state = jnp.where(has, decay * earlier_state + state, state)
        decay = jnp.where(has, decay * earlier_decay, decay)
        distance *= 2
    return passed_along(state, "ctx", sign)


class Box:
    def __init__(self, v):
        self.v = v


class Sequence:
    def __init__(self):
        self.pending = []

    def gate(self, *values):
        boxes = list({id(b): b for b in [*self.pending, *values] if isinstance(b, Box)}.values())
        raw = [value for value in values if not isinstance(value, Box)]
        held, raw = lax.optimization_barrier(([b.v for b in boxes], raw))
        for box, value in zip(boxes, held):
            box.v = value
        raw = iter(raw)
        return [value.v if isinstance(value, Box) else next(raw) for value in values]

    def wait(self, *boxes):
        self.pending = [*self.pending, *boxes]

    def step(self, function, *values):
        out = function(*self.gate(*values))
        if isinstance(out, (tuple, list)):
            out = [Box(value) for value in out]
            self.pending = list(out)
        else:
            out = Box(out)
            self.pending = [out]
        return out

    def send(self, move, value, *args):
        return Box(move(self.gate(value)[0], *args))


class Gather:
    def __init__(self, block, order):
        self.rows, self.width = block.shape
        self.shards = lax.axis_size("shard")
        self.z, self.x = lax.axis_index("shard"), lax.axis_index("ctx")
        self.order = order
        self.own, self.other = [Box(block)], []
        self.pairs = []

    def swap(self):
        self.other.append(self.order.send(swapped, self.own[len(self.other)], "ctx", 1))
        return self.other[-1]

    def turn(self):
        self.own.append(self.order.send(rotated, self.own[-1], "shard", 1))
        return self.own[-1]

    def turn_pair(self):
        if not self.pairs:
            self.pairs.append(
                self.order.step(lambda one, two: jnp.stack([one, two]), self.own[0], self.other[0])
            )
        self.pairs.append(self.order.send(rotated, self.pairs[-1], "shard", 1))
        return self.pairs[-1]

    def whole(self):
        whole = jnp.zeros((self.shards, 2, self.rows, self.width), F32)

        def put(whole, piece, step, span):
            owner = (self.z - step) % self.shards
            piece = piece.reshape(1, -1, self.rows, self.width)
            return lax.dynamic_update_slice(whole, piece, (owner, span, 0, 0))

        for step in range(self.shards):
            own, other = (
                self.pairs[step].v if self.pairs else (self.own[step].v, self.other[step].v)
            )
            whole = put(put(whole, own, step, self.x), other, step, 1 - self.x)
        return Box(whole.reshape(-1, self.width))


def gather_plain(block):
    return lax.all_gather(block, ("shard", "ctx"), axis=0, tiled=True)


def over_shard(rows):
    shards, count, width = rows.shape
    return lax.psum_scatter(
        rows.reshape(shards * count, width), "shard", scatter_dimension=0, tiled=True
    )


class Scatter:
    def __init__(self, kept, sent, order, earlier):
        self.kept, self.sent, self.order, self.earlier = kept, sent, order, earlier
        self.rows = kept.v.shape[1]

    def start_ctx(self):
        self.arriving = self.order.send(swapped, self.sent, "ctx", 1)

    def take_turn(self):
        if self.earlier:
            self.order.wait(self.earlier[-1])

    def end_ctx(self):
        self.take_turn()
        both = self.order.step(lambda one, two: one + two, self.kept, self.arriving)
        self.result = Box(over_shard(self.order.gate(both)[0]))
        self.earlier.append(self.result)

    def start_shard(self):
        self.take_turn()
        both = self.order.step(
            lambda one, two: jnp.concatenate([one, two], axis=1), self.kept, self.sent
        )
        self.both = Box(over_shard(self.order.gate(both)[0]))
        self.earlier.append(self.both)

    def end_shard(self):
        rows = self.rows
        sent = self.order.step(lambda both: both[rows:], self.both)
        self.arriving = self.order.send(swapped, sent, "ctx", 1)
        self.result = self.order.step(
            lambda both, other: both[:rows] + other, self.both, self.arriving
        )


def scatter_plain(total):
    return lax.psum_scatter(total, ("shard", "ctx"), scatter_dimension=0, tiled=True)


class TpSum:
    def __init__(self, kept, sent, order):
        self.order, self.kept, self.arrived = order, kept, None
        self.levels = lax.axis_size("tp") == 4
        if self.levels:
            self.arriving = order.send(swapped, sent, "tp", 1)
        else:
            self.kept = Box(lax.psum(kept.v, "tp"))
            self.arriving = Box(lax.psum(sent.v, "tp"))

    def cross(self):
        if self.levels:
            self.kept = self.order.step(lambda one, two: one + two, self.kept, self.arriving)
            self.arriving = self.order.send(swapped, self.kept, "tp", 2)

    def share(self):
        if self.levels:
            self.kept = self.order.step(lambda one, two: one + two, self.kept, self.arriving)
            self.arriving = self.order.send(swapped, self.kept, "tp", 1)

    def rows(self, kept, arriving):
        first = lax.axis_index("tp") % 2 == 0
        low = jnp.where(first, kept, arriving)
        high = jnp.where(first, arriving, kept)
        return jnp.concatenate([low, high], axis=0)


class SmallSum:
    def __init__(self, value, order, axes):
        self.value, self.order, self.arriving = value, order, None
        self.bits = []
        if any(lax.axis_size(axis) & (lax.axis_size(axis) - 1) for axis in axes):
            self.value = Box(lax.psum(value.v, axes))
            return
        for axis in axes:
            bit = 1
            while bit < lax.axis_size(axis):
                self.bits.append((axis, bit))
                bit *= 2

    def advance(self):
        if self.arriving is not None:
            self.value = self.order.step(lambda one, two: one + two, self.value, self.arriving)
            self.arriving = None
        if self.bits:
            self.arriving = self.order.send(swapped, self.value, *self.bits.pop(0))
            return True
        return False


def row_of(table, index):
    return table[index : index + 1, :]


def tile_scan(decay, value, reverse):
    rows, width = decay.shape
    decay = decay.reshape(rows // 8, 8, width)
    value = value.reshape(rows // 8, 8, width)
    place = lax.broadcasted_iota(jnp.int32, decay.shape, 1)
    for step in (1, 2, 4):
        shift = 8 - step if reverse else step
        inside = place < 8 - step if reverse else place >= step
        other_decay = jnp.where(inside, pltpu.roll(decay, shift, 1), 1.0)
        other_value = jnp.where(inside, pltpu.roll(value, shift, 1), 0.0)
        value = value + decay * other_value
        decay = decay * other_decay
    return decay.reshape(rows, width), value.reshape(rows, width)


def chain_tiles(decay_ref, value_ref, decay_carry, value_carry, reverse):
    tiles = decay_ref.shape[0] // 8
    edge = 0 if reverse else 7
    for step in range(tiles):
        tile = tiles - 1 - step if reverse else step
        rows = slice(tile * 8, tile * 8 + 8)
        decay, value = decay_ref[rows, :], value_ref[rows, :]
        value = value + decay * value_carry
        decay = decay * decay_carry
        decay_ref[rows, :], value_ref[rows, :] = decay, value
        decay_carry = jnp.broadcast_to(decay[edge : edge + 1, :], decay.shape)
        value_carry = jnp.broadcast_to(value[edge : edge + 1, :], value.shape)
    return decay_carry, value_carry


def forward_kernel(
    branch_ref, edge_ref, taps_ref, table_ref, gate_ref,
    conv_ref, a_ref, i_ref, cumul_ref, state_ref, pair_ref,
    padded, carry,
):
    rows, width = branch_ref.shape
    blocks = gate_ref.shape[0]
    block_width = width // blocks
    taps = taps_ref.shape[0]

    @pl.when(pl.program_id(0) == 0)
    def _():
        padded[0:8, :] = edge_ref[...]
        carry[0] = jnp.ones((8, width), F32)
        carry[1] = jnp.zeros((8, width), F32)

    padded[8 : 8 + rows, :] = branch_ref[...]
    conv = jnp.broadcast_to(table_ref[0:1, :], (rows, width))
    for tap in range(taps):
        conv = conv + taps_ref[tap : tap + 1, :] * padded[8 - tap : 8 - tap + rows, :]
    padded[0:8, :] = branch_ref[rows - 8 : rows, :]
    conv_ref[...] = conv
    for block in range(blocks):
        columns = slice(block * block_width, (block + 1) * block_width)
        both = three_pass(conv[:, columns], gate_ref[block], ((1,), (0,)))
        a_rate = jax.nn.sigmoid(both[:, :block_width] + table_ref[1:2, columns])
        i_rate = jax.nn.sigmoid(both[:, block_width:] + table_ref[2:3, columns])
        decay, scale_in = decay_parts(a_rate, table_ref[3:4, columns])
        decay, value = tile_scan(decay, scale_in * i_rate * conv[:, columns], False)
        a_ref[:, columns] = a_rate
        i_ref[:, columns] = i_rate
        cumul_ref[:, columns] = decay
        state_ref[:, columns] = value
    carry[0], carry[1] = chain_tiles(cumul_ref, state_ref, carry[0], carry[1], False)
    pair_ref[...] = carry[...]


def backward_kernel(pre_ref, state_ref, a_ref, table_ref, *refs, chunks):
    mixed_refs = refs[:chunks]
    gate_grad_ref, suffix_ref, adjoint_ref, pair_ref, padded, carry = refs[chunks:]
    rows, width = pre_ref.shape
    chunk = (pl.num_programs(0) - 1 - pl.program_id(0)) * chunks // pl.num_programs(0)

    @pl.when(pl.program_id(0) == 0)
    def _():
        padded[rows : rows + 8, :] = jnp.ones((8, width), F32)
        carry[0] = jnp.ones((8, width), F32)
        carry[1] = jnp.zeros((8, width), F32)

    act, slope = gelu_parts(pre_ref[...])
    grad_mixed = mixed_refs[0][...]
    for place in range(1, chunks):
        grad_mixed = jnp.where(chunk == place, mixed_refs[place][...], grad_mixed)
    gate_grad_ref[...] = grad_mixed * state_ref[...] * slope
    decay = jnp.exp(-DECAY_CONST * a_ref[...] * table_ref[3:4, :])
    padded[0:rows, :] = decay
    shifted = padded[1 : rows + 1, :]
    padded[rows : rows + 8, :] = decay[0:8, :]
    shifted, value = tile_scan(shifted, grad_mixed * act, True)
    suffix_ref[...] = shifted
    adjoint_ref[...] = value
    carry[0], carry[1] = chain_tiles(suffix_ref, adjoint_ref, carry[0], carry[1], True)
    pair_ref[...] = carry[...] * decay[0:1, :][None]


def gradient_kernel(
    suffix_ref, adjoint_ref, conv_ref, a_ref, i_ref, state_ref, before_ref, branch_ref,
    incoming_ref, entry_ref, taps_ref, table_ref, gate_ref,
    branch_grad_ref, head_ref, sums_ref, gate_grad_ref,
    padded, shifted,
):
    rows, width = conv_ref.shape
    blocks = gate_ref.shape[0]
    block_width = width // blocks
    taps = taps_ref.shape[0]
    step, steps = pl.program_id(0), pl.num_programs(0)

    @pl.when(step == 0)
    def _():
        padded[rows : rows + 8, :] = jnp.zeros((8, width), F32)
        sums_ref[...] = jnp.zeros_like(sums_ref)
        gate_grad_ref[...] = jnp.zeros_like(gate_grad_ref)

    shifted[8 : 8 + rows, :] = state_ref[...]
    shifted[0:8, :] = jnp.where(step == steps - 1, entry_ref[...], before_ref[...])

    def total(values):
        return jnp.sum(values, axis=0, keepdims=True)

    for block in range(blocks):
        columns = slice(block * block_width, (block + 1) * block_width)
        adjoint = adjoint_ref[:, columns] + suffix_ref[:, columns] * incoming_ref[0:1, columns]
        conv, a_rate, i_rate = conv_ref[:, columns], a_ref[:, columns], i_ref[:, columns]
        soft_lambda = table_ref[3:4, columns]
        decay, scale_in = decay_parts(a_rate, soft_lambda)
        before = shifted[7 : 7 + rows, columns]
        weighted = adjoint * i_rate
        grad_log = adjoint * before * decay - weighted * conv * (decay * decay) / scale_in
        rate_part = grad_log * (-DECAY_CONST * a_rate)
        grad_a = rate_part * soft_lambda * (1.0 - a_rate)
        grad_i = weighted * scale_in * conv * (1.0 - i_rate)
        sums_ref[0:1, columns] += total(rate_part)
        sums_ref[1:2, columns] += total(grad_a)
        sums_ref[2:3, columns] += total(grad_i)
        both = jnp.concatenate([grad_a, grad_i], axis=1)
        gate_grad_ref[block] += three_pass(conv, both, ((0,), (0,)))
        back = three_pass(both, gate_ref[block], ((1,), (1,)))
        padded[0:rows, columns] = weighted * scale_in + back
    grad_conv = padded[0:rows, :]
    sums_ref[3:4, :] += total(grad_conv)
    head_ref[...] = grad_conv[0:8, :]
    branch = branch_ref[...]
    branch_grad = jnp.zeros((rows, width), F32)
    for tap in range(taps):
        moved = padded[tap : tap + rows, :]
        branch_grad = branch_grad + taps_ref[tap : tap + 1, :] * moved
        sums_ref[4 + tap : 5 + tap, :] += total(moved * branch)
    branch_grad_ref[...] = branch_grad
    padded[rows : rows + 8, :] = grad_conv[0:8, :]


def block_rows(rows):
    return 256 if rows % 1024 == 0 else rows // 4 if rows % 32 == 0 else rows


def fixed(*shape):
    return pl.BlockSpec(shape, lambda i: (0,) * len(shape))


def shaped(*shape):
    return jax.ShapeDtypeStruct(shape, F32)


def run_forward(branch, edges, taps, table, gates):
    rows, width = branch.shape
    step = block_rows(rows)
    moving = pl.BlockSpec((step, width), lambda i: (i, 0))
    return pl.pallas_call(
        forward_kernel,
        grid=(rows // step,),
        in_specs=[
            moving, fixed(8, width), fixed(*taps.shape), fixed(*table.shape), fixed(*gates.shape)
        ],
        out_specs=[moving] * 5 + [fixed(2, 8, width)],
        out_shape=[shaped(rows, width)] * 5 + [shaped(2, 8, width)],
        scratch_shapes=[pltpu.VMEM((step + 8, width), F32), pltpu.VMEM((2, 8, width), F32)],
        compiler_params=pltpu.CompilerParams(vmem_limit_bytes=VMEM_BYTES),
    )(branch, edges, taps, table, gates)


def run_backward(grad_mixed, gate_pre, rec_state, a_rate, table):
    rows, width = gate_pre.shape
    step = block_rows(rows)
    last, chunks = rows // step - 1, len(grad_mixed)
    each = rows // step // chunks
    moving = pl.BlockSpec((step, width), lambda i: (last - i, 0))

    def of_chunk(place):
        return pl.BlockSpec(
            (step, width), lambda i: (jnp.clip(last - i - place * each, 0, each - 1), 0)
        )

    return pl.pallas_call(
        functools.partial(backward_kernel, chunks=chunks),
        grid=(rows // step,),
        in_specs=[moving] * 3
        + [fixed(*table.shape)]
        + [of_chunk(place) for place in range(chunks)],
        out_specs=[moving] * 3 + [fixed(2, 8, width)],
        out_shape=[shaped(rows, width)] * 3 + [shaped(2, 8, width)],
        scratch_shapes=[pltpu.VMEM((step + 8, width), F32), pltpu.VMEM((2, 8, width), F32)],
        compiler_params=pltpu.CompilerParams(vmem_limit_bytes=VMEM_BYTES),
    )(gate_pre, rec_state, a_rate, table, *grad_mixed)


def run_gradient(
    suffix, adjoint, conv_out, a_rate, i_rate, rec_state, branch, incoming, entry, taps, table, gates
):
    rows, width = branch.shape
    step = block_rows(rows)
    last = rows // step - 1
    moving = pl.BlockSpec((step, width), lambda i: (last - i, 0))
    before = pl.BlockSpec(
        (8, width), lambda i: (jnp.maximum((last - i) * (step // 8) - 1, 0), 0)
    )
    return pl.pallas_call(
        gradient_kernel,
        grid=(rows // step,),
        in_specs=[moving] * 6
        + [before, moving, fixed(8, width), fixed(8, width)]
        + [fixed(*taps.shape), fixed(*table.shape), fixed(*gates.shape)],
        out_specs=[moving, fixed(8, width), fixed(8, width), fixed(*gates.shape)],
        out_shape=[
            shaped(rows, width), shaped(8, width), shaped(8, width), shaped(*gates.shape)
        ],
        scratch_shapes=[pltpu.VMEM((step + 8, width), F32), pltpu.VMEM((step + 8, width), F32)],
        compiler_params=pltpu.CompilerParams(vmem_limit_bytes=VMEM_BYTES),
    )(
        suffix, adjoint, conv_out, a_rate, i_rate, rec_state, rec_state, branch,
        incoming, entry, taps, table, gates,
    )


def product_kernel(span_ref, *refs, count, wide, split):
    left_refs, right_refs = refs[:count], refs[count : count + count * wide]
    outs, (high, low) = refs[count + count * wide : -2], refs[-2:]
    chunk, width = right_refs[0].shape

    @pl.when(pl.program_id(0) == 0)
    def _():
        for place, ref in enumerate(right_refs):
            row, column = place // wide * chunk, place % wide * width
            span = (slice(row, row + chunk), slice(column, column + width))
            high[span], low[span] = halves(ref[...])

    product = None
    for place, ref in enumerate(left_refs):
        span = slice(place * chunk, (place + 1) * chunk)
        left_high, left_low = halves(ref[...])

        def part(one, two):
            return lax.dot_general(
                one, two[span, :], (((0,), (0,)), ((), ())), preferred_element_type=F32
            )

        term = part(left_high, high) + (part(left_high, low) + part(left_low, high))
        product = term if product is None else product + term
    if not split:
        outs[0][...] = product
        return
    rows = product.shape[0] // 2
    first = span_ref[0] == 0
    zero, one = product[:rows], product[rows:]
    outs[0][0] = jnp.where(first, zero, one)
    outs[1][0] = jnp.where(first, one, zero)


def run_product(lefts, rights, wide, split):
    count = len(lefts)
    (chunk, depth), width = lefts[0].shape, rights[0].shape[1]
    shards = lax.axis_size("shard")
    rows = depth // (2 * shards)
    span = lax.axis_index("ctx").astype(jnp.int32).reshape(1)
    if split:
        out_specs = [pl.BlockSpec((1, rows, wide * width), lambda i, span: (i, 0, 0))] * 2
        out_shape = [shaped(shards, rows, wide * width)] * 2
    else:
        out_specs = [pl.BlockSpec((2 * rows, wide * width), lambda i, span: (i, 0))]
        out_shape = [shaped(depth, wide * width)]
    return pl.pallas_call(
        functools.partial(product_kernel, count=count, wide=wide, split=split),
        grid_spec=pltpu.PrefetchScalarGridSpec(
            num_scalar_prefetch=1,
            grid=(shards,),
            in_specs=[pl.BlockSpec((chunk, 2 * rows), lambda i, span: (0, i))] * count
            + [
                pl.BlockSpec(
                    (chunk, width), lambda i, span: (0, 0), pipeline_mode=pl.Buffered(1)
                )
            ]
            * (count * wide),
            out_specs=out_specs,
            scratch_shapes=[pltpu.VMEM((count * chunk, wide * width), BF16)] * 2,
        ),
        out_shape=out_shape,
        compiler_params=pltpu.CompilerParams(vmem_limit_bytes=VMEM_BYTES),
    )(span, *lefts, *rights)


def dot_parts(left_high, left_low, right_high, right_low, dims):
    def part(one, two):
        return lax.dot_general(one, two, (dims, ((), ())), preferred_element_type=F32)

    return part(left_high, right_high) + (part(left_high, right_low) + part(left_low, right_high))


def across_kernel(side_ref, *refs, count):
    lefts, rights = refs[:count], refs[count : 2 * count]
    kept_ref, sent_ref = refs[2 * count : 2 * count + 2]
    scratch = refs[2 * count + 2 :]

    @pl.when(pl.program_id(0) == 0)
    def _():
        for place, ref in enumerate(lefts):
            scratch[2 * place][...], scratch[2 * place + 1][...] = halves(ref[...])

    product = None
    for place in range(count):
        term = dot_parts(
            scratch[2 * place][...], scratch[2 * place + 1][...],
            *halves(rights[place][...]), ((1,), (1,)),
        )
        product = term if product is None else product + term
    half = kept_ref.shape[0]
    first = side_ref[0] == 0
    low, high = product[:half], product[half:]
    kept_ref[...] = jnp.where(first, low, high)
    sent_ref[...] = jnp.where(first, high, low)


def run_across(lefts, rights, chunk, rows):
    count, depth = len(lefts), rights[0].shape[0]
    step = 512 if depth % 512 == 0 else depth
    side = (lax.axis_index("tp") % 2).astype(jnp.int32).reshape(1)
    half = pl.BlockSpec((rows // 2, step), lambda i, side: (0, i))
    widths = [left.shape[1] for left in lefts]
    return pl.pallas_call(
        functools.partial(across_kernel, count=count),
        grid_spec=pltpu.PrefetchScalarGridSpec(
            num_scalar_prefetch=1,
            grid=(depth // step,),
            in_specs=[pl.BlockSpec((rows, w), lambda i, side: (chunk, 0)) for w in widths]
            + [pl.BlockSpec((step, w), lambda i, side: (i, 0)) for w in widths],
            out_specs=[half, half],
            scratch_shapes=[pltpu.VMEM((rows, w), BF16) for w in widths for _ in range(2)],
        ),
        out_shape=[shaped(rows // 2, depth)] * 2,
        compiler_params=pltpu.CompilerParams(vmem_limit_bytes=VMEM_BYTES),
    )(side, *lefts, *rights)


def up_product(value, pre):
    act, slope = gelu_parts(pre)
    return act * value, act, slope * value


def hidden_product(grad_hidden, act, slope_up):
    return grad_hidden * slope_up, grad_hidden * act


def norm_parts(rows):
    inv = lax.rsqrt(jnp.mean(rows * rows, axis=1, keepdims=True) + EPSILON)
    return inv, rows * inv


def norm_back(grad_normed, normed_hat, inv_scale, gain):
    grad_hat = grad_normed * gain
    inner = jnp.mean(grad_hat * normed_hat, axis=1, keepdims=True)
    return (inv_scale * (grad_hat - normed_hat * inner), jnp.sum(grad_normed * normed_hat, axis=0))


def on_device(
    inputs,
    lengths,
    rec_proj,
    gate_proj,
    out_proj,
    ffn_gate,
    ffn_up,
    ffn_down,
    conv_weight,
    conv_bias,
    a_gate,
    i_gate,
    a_bias,
    i_bias,
    lambda_param,
    rec_norm,
    ffn_norm,
    cotangent,
):
    seqs_here, span_len, width_model = inputs.shape
    row_count = seqs_here * span_len
    taps = conv_weight.shape[0]
    width_rec, width_ffn = rec_proj.shape[1], ffn_gate.shape[1]
    chunks = 4
    chunk_rows = row_count // chunks

    def rows_of(values, chunk):
        return values[chunk * chunk_rows : (chunk + 1) * chunk_rows]

    position = lax.axis_index("ctx") * span_len + jnp.arange(span_len, dtype=jnp.int32)
    valid_mask = position[None, :] < lengths[:, None]
    mask_rows = valid_mask.reshape(row_count, 1).astype(F32)

    two_level = lax.axis_size("ctx") == 2
    order = Sequence()
    chunk_list = list(range(chunks))
    scattered = []

    def weight_grad(lefts, rights, wide=1, split=True):
        count = len(lefts)
        if not two_level:
            total = order.step(
                lambda *a: matmul_tn(
                    jnp.concatenate(a[:count]),
                    jnp.concatenate(a[count:], axis=1 if wide > 1 else 0),
                ),
                *lefts, *rights,
            )
            return Box(scatter_plain(total.v))
        out = order.step(
            lambda *a: run_product(a[:count], a[count:], wide, split), *lefts, *rights
        )
        if split:
            return Scatter(*out, order, scattered)
        if scattered:
            order.wait(scattered[-1])
        scattered.append(Box(scatter_plain(order.gate(out[0])[0])))
        return scattered[-1]

    def start_ctx(grad):
        if isinstance(grad, Scatter):
            grad.start_ctx()

    def end_ctx(grad):
        if isinstance(grad, Scatter):
            grad.end_ctx()
            return grad.result
        return grad

    flat_in = inputs.reshape(row_count, width_model)
    flat_cot = cotangent.reshape(row_count, width_model)
    soft_lambda = jax.nn.softplus(-lambda_param)
    table = jnp.concatenate(
        [jnp.stack([conv_bias, a_bias, i_bias, soft_lambda]), jnp.zeros((4, width_rec), F32)]
    )
    gates = jnp.concatenate([a_gate, i_gate], axis=2)

    def norm_all(rows, gain):
        inv, hat = norm_parts(rows)
        return inv, hat * gain

    blocks = (rec_proj, gate_proj, out_proj, ffn_gate, ffn_up, ffn_down)
    turns = lax.axis_size("shard") - 1
    direct = two_level and turns == 3 and chunks == 4

    def partial_sum(lefts, weights, c):
        kept, sent = order.step(
            lambda *a: run_across(a[: len(lefts)], a[len(lefts) :], c, chunk_rows),
            *lefts, *weights,
        )
        return TpSum(kept, sent, order)

    def gathered(block, *earlier):
        order.wait(*earlier)
        return Box(gather_plain(order.gate(block)[0]))

    fg_weight = Box(gather_plain(ffn_gate))
    pending = []

    def tick(*sends):
        order.wait(*pending)
        pending[:] = [send() for send in sends]

    if direct:
        rec, gbr, out = (Gather(block, order) for block in blocks[:3])
        first = [gbr.swap(), out.swap(), rec.swap()]
        for _ in range(turns):
            tick(rec.turn)
        tick()
        order.wait(first[0], first[1])
        tick(gbr.turn_pair, *([rec.swap] * turns))
        late = pending[1:]
        del pending[1:]
        inv_one, normed_one = order.step(norm_all, flat_in, rec_norm)
        tick(gbr.turn_pair)
        order.wait(*late)
        rec_weight = rec.whole()
    else:
        rec_weight, gbr_weight, out_weight = (Box(gather_plain(block)) for block in blocks[:3])
        inv_one, normed_one = order.step(norm_all, flat_in, rec_norm)
    branch = order.step(matmul, normed_one, rec_weight)
    branch_end = order.step(lambda branch: branch[row_count - (taps - 1) :], branch)
    left_edges = order.send(passed_along, branch_end, "ctx", 1)
    if direct:
        tick(gbr.turn_pair)
        tick(out.turn_pair)
        gbr_weight = gbr.whole()
    gate_pre = order.step(matmul, normed_one, gbr_weight)
    if direct:
        tick(out.turn_pair)
    conv_out, a_rate, i_rate, cumul, local_state, pair = order.step(
        lambda branch, edges, *rest: run_forward(
            branch, jnp.pad(edges, ((8 - (taps - 1), 0), (0, 0))), *rest
        ),
        branch, left_edges, conv_weight, table, gates,
    )
    entry = Box(carried_in(pair.v[0], pair.v[1], 1))
    if direct:
        tick(out.turn_pair)
    fu_weight = gathered(ffn_up, fg_weight)

    def mix(local_state, cumul, entry, gate_pre):
        rec_state = local_state + cumul * entry[0:1]
        return rec_state, rec_state * gelu(gate_pre)

    rec_state, mixed_rows = order.step(mix, local_state, cumul, entry, gate_pre)
    if direct:
        tick()
        out_weight = out.whole()
    mix_sums, after_mix, inv_two, normed_two, gate_in, hidden, acts = (
        [None] * chunks for _ in range(7)
    )

    def start_mix(c):
        mix_sums[c] = partial_sum([mixed_rows], [out_weight], c)

    def take_mix(c):
        def norm_chunk(rows, kept, arriving, gain):
            rows = rows_of(rows, c) + mix_sums[c].rows(kept, arriving)
            inv, hat = norm_parts(rows)
            return rows, inv, hat * gain

        after_mix[c], inv_two[c], normed_two[c] = order.step(
            norm_chunk, flat_in, mix_sums[c].kept, mix_sums[c].arriving, ffn_norm
        )

    def run_gate(c):
        gate_in[c] = order.step(matmul, normed_two[c], fg_weight)

    def run_up(c):
        hidden[c], *acts[c] = order.step(
            lambda left, weight, pre: up_product(matmul(left, weight), pre),
            normed_two[c], fu_weight, gate_in[c],
        )

    grad_result = [None] * chunks

    def mask_chunk(c):
        grad_result[c] = order.step(
            lambda rows, mask: rows_of(rows, c) * rows_of(mask, c), flat_cot, mask_rows
        )

    start_mix(0)
    start_mix(1)
    mix_sums[0].cross()
    start_mix(2)
    mix_sums[1].cross()
    start_mix(3)
    for c in chunk_list:
        mask_chunk(c)
    mix_sums[0].share()
    mix_sums[2].cross()
    take_mix(0)
    run_gate(0)
    mix_sums[1].share()
    mix_sums[3].cross()
    take_mix(1)
    run_gate(1)
    fd_weight = gathered(ffn_down, fu_weight)
    run_up(0)
    mix_sums[2].share()
    run_up(1)
    take_mix(2)
    run_gate(2)
    run_up(2)
    mix_sums[3].share()
    take_mix(3)
    run_gate(3)
    run_up(3)

    ffn_sums, back_sums, grad_pre, grad_up = ([None] * chunks for _ in range(4))
    grad_after_mix, norm_two_sums, grad_mixed = ([None] * chunks for _ in range(3))
    block_out = None

    def start_ffn(c):
        ffn_sums[c] = partial_sum([hidden[c]], [fd_weight], 0)

    def take_ffn(c):
        nonlocal block_out

        def place(rows, kept, arriving, mask, block_out=None):
            rows = (rows + ffn_sums[c].rows(kept, arriving)) * rows_of(mask, c)
            if block_out is None:
                block_out = jnp.zeros((row_count, width_model), F32)
            return lax.dynamic_update_slice(block_out, rows, (c * chunk_rows, 0))

        block_out = order.step(
            place, after_mix[c], ffn_sums[c].kept, ffn_sums[c].arriving, mask_rows,
            *([block_out] if block_out else []),
        )

    def run_hidden(c):
        grad_pre[c], grad_up[c] = order.step(
            lambda left, weight, *acts: hidden_product(matmul(left, weight), *acts),
            grad_result[c], fd_weight, *acts[c],
        )

    def start_back(c):
        back_sums[c] = partial_sum([grad_pre[c], grad_up[c]], [fg_weight, fu_weight], 0)

    def take_back(c):
        def back(rows, after, inv, kept, arriving, gain):
            from_two, norm_sum = norm_back(
                back_sums[c].rows(kept, arriving), after * inv, inv, gain
            )
            return rows + from_two, norm_sum

        grad_after_mix[c], norm_two_sums[c] = order.step(
            back, grad_result[c], after_mix[c], inv_two[c],
            back_sums[c].kept, back_sums[c].arriving, ffn_norm,
        )
        grad_mixed[c] = order.step(matmul, grad_after_mix[c], out_weight)

    start_ffn(0)
    start_ffn(1)
    ffn_sums[0].cross()
    ffn_sums[1].cross()
    grad_fd = weight_grad(grad_result, hidden, split=False)
    run_hidden(3)
    start_back(3)
    ffn_sums[0].share()
    run_hidden(2)
    back_sums[3].cross()
    take_ffn(0)
    start_back(2)
    ffn_sums[1].share()
    run_hidden(1)
    back_sums[2].cross()
    take_ffn(1)
    start_back(1)
    back_sums[3].share()
    run_hidden(0)
    back_sums[1].cross()
    take_back(3)
    start_back(0)
    back_sums[2].share()
    grad_fg = weight_grad(normed_two, grad_pre, split=False)
    back_sums[0].cross()
    take_back(2)
    start_ffn(2)
    back_sums[1].share()
    start_ffn(3)
    ffn_sums[2].cross()
    take_back(1)
    grad_fu = weight_grad(normed_two, grad_up)
    start_ctx(grad_fu)
    back_sums[0].share()
    ffn_sums[3].cross()
    take_back(0)

    grad_gate_pre, suffix, local_adjoint, back_pair = order.step(
        lambda pre, state, rate, table, *mixed: run_backward(mixed, pre, state, rate, table),
        gate_pre, rec_state, a_rate, table, *grad_mixed,
    )
    incoming = Box(carried_in(back_pair.v[0], back_pair.v[1], -1))
    grad_branch, head, sums, grad_gates = order.step(
        run_gradient,
        suffix, local_adjoint, conv_out, a_rate, i_rate, rec_state, branch, incoming, entry,
        conv_weight, table, gates,
    )
    head = order.step(lambda head: head[: taps - 1], head)
    right_edges = order.send(passed_along, head, "ctx", -1)

    def tail_rows(grad_branch, right_edges, conv_weight):
        tail = grad_branch[row_count - (taps - 1) :]
        padded_edges = jnp.concatenate([jnp.zeros_like(right_edges), right_edges])
        for tap in range(1, taps):
            tail = tail + conv_weight[tap] * padded_edges[tap : tap + taps - 1]
        return lax.dynamic_update_slice(grad_branch, tail, (row_count - (taps - 1), 0))

    one_sums = [None] * chunks

    def start_one(c):
        one_sums[c] = partial_sum([grad_branch, grad_gate_pre], [rec_weight, gbr_weight], c)

    input_grad = None

    def take_one(c):
        nonlocal input_grad

        def back(rows, after, inv, kept, arriving, gain, grads=None):
            inv = rows_of(inv, c)
            from_one, _ = norm_back(
                one_sums[c].rows(kept, arriving), rows_of(after, c) * inv, inv, gain
            )
            if grads is None:
                grads = jnp.zeros((row_count, width_model), F32)
            return lax.dynamic_update_slice(grads, rows + from_one, (c * chunk_rows, 0))

        input_grad = order.step(
            back, grad_after_mix[c], flat_in, inv_one,
            one_sums[c].kept, one_sums[c].arriving, rec_norm,
            *([input_grad] if input_grad else []),
        )

    def small_parts(sums, head, left_edges, grad_gates, lambda_param, *norm_two):
        padded_head = jnp.concatenate([left_edges, jnp.zeros_like(left_edges)])
        edge = taps - 1
        grad_taps = [sums[4]] + [
            sums[4 + tap] + jnp.sum(head * padded_head[edge - tap : 2 * edge - tap], axis=0)
            for tap in range(1, taps)
        ]
        grad_lambda = sums[0] * -jax.nn.sigmoid(-lambda_param)
        vectors = jnp.stack([*grad_taps, sums[1], sums[2], sums[3], grad_lambda])
        return jnp.concatenate(
            [grad_gates.reshape(-1, 128), vectors.reshape(-1, 128), sum(norm_two).reshape(-1, 128)]
        )

    start_one(0)
    ffn_sums[2].share()
    start_one(1)
    one_sums[0].cross()
    grad_fu = end_ctx(grad_fu)
    take_ffn(2)
    grad_branch = order.step(tail_rows, grad_branch, right_edges, conv_weight)
    grad_recs = weight_grad([normed_one], [grad_branch, grad_gate_pre], wide=2)
    rec_parts = grad_recs
    start_ctx(grad_recs)
    ffn_sums[3].share()
    start_one(2)
    one_sums[1].cross()
    take_ffn(3)
    small = order.step(
        small_parts, sums, head, left_edges, grad_gates, lambda_param, *norm_two_sums
    )
    small = SmallSum(small, order, ("ctx", "shard"))
    small.advance()
    start_one(3)
    one_sums[0].share()
    grad_out_proj = weight_grad(
        grad_after_mix, order.step(lambda rows: [rows_of(rows, c) for c in chunk_list], mixed_rows)
    )
    one_sums[2].cross()
    take_one(0)
    small.advance()
    block_out = block_out.v.reshape(seqs_here, span_len, width_model)

    if two_level:
        span = lax.axis_index("ctx")

        def gain_sums(kept, sent, gain, rec_weight, gbr_weight):
            def rows_sum(grads, which):
                total = 0.0
                for place, weight in enumerate((rec_weight, gbr_weight)):
                    split = weight.reshape(turns + 1, 2, -1, width_rec)
                    split = lax.dynamic_index_in_dim(split, which, 1, keepdims=False)
                    grad = grads[:, :, place * width_rec : (place + 1) * width_rec]
                    total = total + jnp.sum(grad * split, axis=2)
                return total

            kept, sent = rows_sum(kept, span), rows_sum(sent, 1 - span)
            both = jnp.stack(
                [jnp.where(span == 0, kept, sent), jnp.where(span == 0, sent, kept)], axis=1
            )
            return (both.reshape(-1) / gain).reshape(-1, 128)

        norm_one_sum = order.step(
            gain_sums, rec_parts.kept, rec_parts.sent, rec_norm, rec_weight, gbr_weight
        )
    else:
        def gain_sums(grads, more, normed, gain, first, second):
            back = matmul_nt(grads, first) + matmul_nt(more, second)
            return (jnp.sum(back * normed, axis=0) / gain).reshape(-1, 128)

        norm_one_sum = order.step(
            gain_sums, grad_branch, grad_gate_pre, normed_one, rec_norm, rec_weight, gbr_weight
        )
    tiny = SmallSum(norm_one_sum, order, ("tp", "ctx", "shard"))
    one_sums[1].share()
    tiny.advance()
    one_sums[3].cross()
    take_one(1)
    tiny.advance()
    grad_recs = end_ctx(grad_recs)
    start_ctx(grad_out_proj)
    small.advance()
    one_sums[2].share()
    tiny.advance()
    take_one(2)
    tiny.advance()
    small.advance()
    grad_out_proj = end_ctx(grad_out_proj)
    tiny.advance()
    one_sums[3].share()
    tiny.advance()
    take_one(3)
    for left in (small, tiny):
        while left.advance():
            pass
    input_grad = input_grad.v.reshape(seqs_here, span_len, width_model)
    small = small.value.v
    sum_norm_one = tiny.value.v.reshape(-1)
    gate_rows = gates.size // 128
    vector_rows = (taps + 4) * width_rec // 128
    sum_gates = small[:gate_rows].reshape(gates.shape)
    vectors = small[gate_rows : gate_rows + vector_rows].reshape(taps + 4, width_rec)
    sum_norm_two = small[gate_rows + vector_rows :].reshape(-1)
    sum_conv_weight = vectors[:taps]
    sum_a_bias, sum_i_bias, sum_conv_bias, sum_lambda = (vectors[taps + k] for k in range(4))
    grad_recs, grad_out_proj, grad_fg, grad_fu, grad_fd = (
        grad.v for grad in (grad_recs, grad_out_proj, grad_fg, grad_fu, grad_fd)
    )
    grad_rec_proj, grad_gate_proj = grad_recs[:, :width_rec], grad_recs[:, width_rec:]
    block_width = a_gate.shape[2]
    return (
        block_out,
        input_grad,
        grad_rec_proj,
        grad_gate_proj,
        grad_out_proj,
        grad_fg,
        grad_fu,
        grad_fd,
        sum_conv_weight,
        sum_conv_bias,
        sum_gates[:, :, :block_width],
        sum_gates[:, :, block_width:],
        sum_a_bias,
        sum_i_bias,
        sum_lambda,
        sum_norm_one,
        sum_norm_two,
    )


def solution(mesh):
    placed = (
        P("shard", "ctx", None),
        P("shard"),
        P(("shard", "ctx"), "tp"),
        P(("shard", "ctx"), "tp"),
        P(("shard", "ctx"), "tp"),
        P(("shard", "ctx"), "tp"),
        P(("shard", "ctx"), "tp"),
        P(("shard", "ctx"), "tp"),
        P(None, "tp"),
        P("tp"),
        P("tp", None, None),
        P("tp", None, None),
        P("tp"),
        P("tp"),
        P("tp"),
        P(),
        P(),
        P("shard", "ctx", None),
    )
    return jax.shard_map(
        on_device,
        mesh=mesh,
        in_specs=placed,
        out_specs=(
            P("shard", "ctx", None),
            P("shard", "ctx", None),
            P(("shard", "ctx"), "tp"),
            P(("shard", "ctx"), "tp"),
            P(("shard", "ctx"), "tp"),
            P(("shard", "ctx"), "tp"),
            P(("shard", "ctx"), "tp"),
            P(("shard", "ctx"), "tp"),
            P(None, "tp"),
            P("tp"),
            P("tp", None, None),
            P("tp", None, None),
            P("tp"),
            P("tp"),
            P("tp"),
            P(),
            P(),
        ),
        check_vma=False,
    )
```

```python
import functools

import jax
import jax.numpy as jnp
from jax import lax
from jax.experimental import pallas as pl
from jax.experimental.pallas import tpu as pltpu
from jax.sharding import PartitionSpec as P

HIGH = lax.Precision.HIGH
EPSILON = 1e-06
DECAY_CONST = 8.0
ROOT = 0.7978845608028654
CUBIC = 0.044715
F32 = jnp.float32
BF16 = jnp.bfloat16
VMEM_BYTES = 56 * 1024 * 1024


def matmul(left, right):
    return jnp.dot(left, right, precision=HIGH, preferred_element_type=F32)


def matmul_nt(left, right):
    return lax.dot_general(
        left, right, (((1,), (1,)), ((), ())), precision=HIGH, preferred_element_type=F32
    )


def matmul_tn(left, right):
    return lax.dot_general(
        left, right, (((0,), (0,)), ((), ())), precision=HIGH, preferred_element_type=F32
    )


def halves(values):
    high = values.astype(BF16)
    return high, (values - high.astype(F32)).astype(BF16)


def three_pass(left, right, dims):
    left_high, left_low = halves(left)
    right_high, right_low = halves(right)

    def part(one, two):
        return lax.dot_general(one, two, (dims, ((), ())), preferred_element_type=F32)

    return part(left_high, right_high) + (part(left_high, right_low) + part(left_low, right_high))


def gelu_parts(values):
    square = values * values
    curve = jnp.tanh(ROOT * values * (1.0 + CUBIC * square))
    act = 0.5 * values * (1.0 + curve)
    slope = 0.5 * (1.0 + curve) + 0.5 * values * (1.0 - curve * curve) * ROOT * (
        1.0 + 3.0 * CUBIC * square
    )
    return act, slope


def gelu(values):
    return 0.5 * values * (1.0 + jnp.tanh(ROOT * values * (1.0 + CUBIC * values * values)))


def expm1_negative(values):
    series = jnp.full_like(values, 1.0)
    for order in range(11, 1, -1):
        series = 1.0 + values * (1.0 / order) * series
    return jnp.where(values > -1.0, values * series, jnp.exp(values) - 1.0)


def decay_parts(a_rate, soft_lambda):
    log_decay = -DECAY_CONST * a_rate * soft_lambda
    return jnp.exp(log_decay), jnp.sqrt(-expm1_negative(2.0 * log_decay))


def passed_along(block, axis, distance):
    devices = range(lax.axis_size(axis))
    route = [(i - distance, i) for i in devices if i - distance in devices]
    return lax.ppermute(block, axis, route)


def rotated(block, axis, distance):
    count = lax.axis_size(axis)
    return lax.ppermute(block, axis, [(i, (i + distance) % count) for i in range(count)])


def swapped(block, axis, bit):
    return lax.ppermute(block, axis, [(i, i ^ bit) for i in range(lax.axis_size(axis))])


def carried_in(decay, state, sign):
    count = lax.axis_size("ctx")
    mine = lax.axis_index("ctx")
    place = mine if sign > 0 else count - 1 - mine
    distance = 1
    while distance < count - 1:
        earlier_decay = passed_along(decay, "ctx", sign * distance)
        earlier_state = passed_along(state, "ctx", sign * distance)
        has = place >= distance
        state = jnp.where(has, decay * earlier_state + state, state)
        decay = jnp.where(has, decay * earlier_decay, decay)
        distance *= 2
    return passed_along(state, "ctx", sign)


class Box:
    def __init__(self, v):
        self.v = v


class Sequence:
    def __init__(self):
        self.pending = []

    def gate(self, *values):
        boxes = list({id(b): b for b in [*self.pending, *values] if isinstance(b, Box)}.values())
        raw = [value for value in values if not isinstance(value, Box)]
        held, raw = lax.optimization_barrier(([b.v for b in boxes], raw))
        for box, value in zip(boxes, held):
            box.v = value
        raw = iter(raw)
        return [value.v if isinstance(value, Box) else next(raw) for value in values]

    def wait(self, *boxes):
        self.pending = [*self.pending, *boxes]

    def step(self, function, *values):
        out = function(*self.gate(*values))
        if isinstance(out, (tuple, list)):
            out = [Box(value) for value in out]
            self.pending = list(out)
        else:
            out = Box(out)
            self.pending = [out]
        return out

    def send(self, move, value, *args):
        return Box(move(self.gate(value)[0], *args))


class Gather:
    def __init__(self, block, order):
        self.rows, self.width = block.shape
        self.shards = lax.axis_size("shard")
        self.z, self.x = lax.axis_index("shard"), lax.axis_index("ctx")
        self.order = order
        self.own, self.other = [Box(block)], []
        self.pairs = []

    def swap(self):
        self.other.append(self.order.send(swapped, self.own[len(self.other)], "ctx", 1))
        return self.other[-1]

    def turn(self):
        self.own.append(self.order.send(rotated, self.own[-1], "shard", 1))
        return self.own[-1]

    def turn_pair(self):
        if not self.pairs:
            self.pairs.append(
                self.order.step(lambda one, two: jnp.stack([one, two]), self.own[0], self.other[0])
            )
        self.pairs.append(self.order.send(rotated, self.pairs[-1], "shard", 1))
        return self.pairs[-1]

    def whole(self):
        whole = jnp.zeros((self.shards, 2, self.rows, self.width), F32)

        def put(whole, piece, step, span):
            owner = (self.z - step) % self.shards
            piece = piece.reshape(1, -1, self.rows, self.width)
            return lax.dynamic_update_slice(whole, piece, (owner, span, 0, 0))

        for step in range(self.shards):
            own, other = (
                self.pairs[step].v if self.pairs else (self.own[step].v, self.other[step].v)
            )
            whole = put(put(whole, own, step, self.x), other, step, 1 - self.x)
        return Box(whole.reshape(-1, self.width))


def gather_plain(block):
    return lax.all_gather(block, ("shard", "ctx"), axis=0, tiled=True)


class Scatter:
    def __init__(self, kept, sent, order):
        self.kept, self.sent, self.order = kept, sent, order
        self.shards = lax.axis_size("shard")

    def start_ctx(self):
        self.arriving = self.order.send(swapped, self.sent, "ctx", 1)

    def start_shard(self):
        z = lax.axis_index("shard")
        parts = self.order.step(
            lambda kept, other: [
                lax.dynamic_index_in_dim(kept, (z + step) % self.shards, 0, keepdims=False)
                + lax.dynamic_index_in_dim(other, (z + step) % self.shards, 0, keepdims=False)
                for step in range(self.shards)
            ],
            self.kept, self.arriving,
        )
        self.mine = parts[0]
        self.parts = [
            self.order.send(rotated, parts[step], "shard", step) for step in range(1, self.shards)
        ]

    def result(self):
        return self.order.step(lambda *parts: sum(parts[1:], parts[0]), self.mine, *self.parts)


class Unsplit:
    def __init__(self, total):
        self.kept = total

    def start_ctx(self):
        pass

    def start_shard(self):
        pass

    def result(self):
        return Box(
            lax.psum_scatter(self.kept.v, ("shard", "ctx"), scatter_dimension=0, tiled=True)
        )


class TpSum:
    def __init__(self, kept, sent, order):
        self.order, self.kept, self.arrived = order, kept, None
        self.levels = lax.axis_size("tp") == 4
        if self.levels:
            self.arriving = order.send(swapped, sent, "tp", 1)
        else:
            self.kept = Box(lax.psum(kept.v, "tp"))
            self.arriving = Box(lax.psum(sent.v, "tp"))

    def cross(self):
        if self.levels:
            self.kept = self.order.step(lambda one, two: one + two, self.kept, self.arriving)
            self.arriving = self.order.send(swapped, self.kept, "tp", 2)

    def share(self):
        if self.levels:
            self.kept = self.order.step(lambda one, two: one + two, self.kept, self.arriving)
            self.arriving = self.order.send(swapped, self.kept, "tp", 1)

    def rows(self, kept, arriving):
        first = lax.axis_index("tp") % 2 == 0
        low = jnp.where(first, kept, arriving)
        high = jnp.where(first, arriving, kept)
        return jnp.concatenate([low, high], axis=0)


class SmallSum:
    def __init__(self, value, order, axes):
        self.value, self.order, self.arriving = value, order, None
        self.bits = []
        if any(lax.axis_size(axis) & (lax.axis_size(axis) - 1) for axis in axes):
            self.value = Box(lax.psum(value.v, axes))
            return
        for axis in axes:
            bit = 1
            while bit < lax.axis_size(axis):
                self.bits.append((axis, bit))
                bit *= 2

    def advance(self):
        if self.arriving is not None:
            self.value = self.order.step(lambda one, two: one + two, self.value, self.arriving)
            self.arriving = None
        if self.bits:
            self.arriving = self.order.send(swapped, self.value, *self.bits.pop(0))
            return True
        return False


def row_of(table, index):
    return table[index : index + 1, :]


def tile_scan(decay, value, reverse):
    rows, width = decay.shape
    decay = decay.reshape(rows // 8, 8, width)
    value = value.reshape(rows // 8, 8, width)
    place = lax.broadcasted_iota(jnp.int32, decay.shape, 1)
    for step in (1, 2, 4):
        shift = 8 - step if reverse else step
        inside = place < 8 - step if reverse else place >= step
        other_decay = jnp.where(inside, pltpu.roll(decay, shift, 1), 1.0)
        other_value = jnp.where(inside, pltpu.roll(value, shift, 1), 0.0)
        value = value + decay * other_value
        decay = decay * other_decay
    return decay.reshape(rows, width), value.reshape(rows, width)


def chain_tiles(decay_ref, value_ref, decay_carry, value_carry, reverse):
    tiles = decay_ref.shape[0] // 8
    edge = 0 if reverse else 7
    for step in range(tiles):
        tile = tiles - 1 - step if reverse else step
        rows = slice(tile * 8, tile * 8 + 8)
        decay, value = decay_ref[rows, :], value_ref[rows, :]
        value = value + decay * value_carry
        decay = decay * decay_carry
        decay_ref[rows, :], value_ref[rows, :] = decay, value
        decay_carry = jnp.broadcast_to(decay[edge : edge + 1, :], decay.shape)
        value_carry = jnp.broadcast_to(value[edge : edge + 1, :], value.shape)
    return decay_carry, value_carry


def forward_kernel(
    branch_ref, edge_ref, taps_ref, table_ref, gate_ref,
    conv_ref, a_ref, i_ref, cumul_ref, state_ref, pair_ref,
    padded, carry,
):
    rows, width = branch_ref.shape
    blocks = gate_ref.shape[0]
    block_width = width // blocks
    taps = taps_ref.shape[0]

    @pl.when(pl.program_id(0) == 0)
    def _():
        padded[0:8, :] = edge_ref[...]
        carry[0] = jnp.ones((8, width), F32)
        carry[1] = jnp.zeros((8, width), F32)

    padded[8 : 8 + rows, :] = branch_ref[...]
    conv = jnp.broadcast_to(table_ref[0:1, :], (rows, width))
    for tap in range(taps):
        conv = conv + taps_ref[tap : tap + 1, :] * padded[8 - tap : 8 - tap + rows, :]
    padded[0:8, :] = branch_ref[rows - 8 : rows, :]
    conv_ref[...] = conv
    for block in range(blocks):
        columns = slice(block * block_width, (block + 1) * block_width)
        both = three_pass(conv[:, columns], gate_ref[block], ((1,), (0,)))
        a_rate = jax.nn.sigmoid(both[:, :block_width] + table_ref[1:2, columns])
        i_rate = jax.nn.sigmoid(both[:, block_width:] + table_ref[2:3, columns])
        decay, scale_in = decay_parts(a_rate, table_ref[3:4, columns])
        decay, value = tile_scan(decay, scale_in * i_rate * conv[:, columns], False)
        a_ref[:, columns] = a_rate
        i_ref[:, columns] = i_rate
        cumul_ref[:, columns] = decay
        state_ref[:, columns] = value
    carry[0], carry[1] = chain_tiles(cumul_ref, state_ref, carry[0], carry[1], False)
    pair_ref[...] = carry[...]


def backward_kernel(pre_ref, state_ref, a_ref, table_ref, *refs, chunks):
    mixed_refs = refs[:chunks]
    gate_grad_ref, suffix_ref, adjoint_ref, pair_ref, padded, carry = refs[chunks:]
    rows, width = pre_ref.shape
    chunk = (pl.num_programs(0) - 1 - pl.program_id(0)) * chunks // pl.num_programs(0)

    @pl.when(pl.program_id(0) == 0)
    def _():
        padded[rows : rows + 8, :] = jnp.ones((8, width), F32)
        carry[0] = jnp.ones((8, width), F32)
        carry[1] = jnp.zeros((8, width), F32)

    act, slope = gelu_parts(pre_ref[...])
    grad_mixed = mixed_refs[0][...]
    for place in range(1, chunks):
        grad_mixed = jnp.where(chunk == place, mixed_refs[place][...], grad_mixed)
    gate_grad_ref[...] = grad_mixed * state_ref[...] * slope
    decay = jnp.exp(-DECAY_CONST * a_ref[...] * table_ref[3:4, :])
    padded[0:rows, :] = decay
    shifted = padded[1 : rows + 1, :]
    padded[rows : rows + 8, :] = decay[0:8, :]
    shifted, value = tile_scan(shifted, grad_mixed * act, True)
    suffix_ref[...] = shifted
    adjoint_ref[...] = value
    carry[0], carry[1] = chain_tiles(suffix_ref, adjoint_ref, carry[0], carry[1], True)
    pair_ref[...] = carry[...] * decay[0:1, :][None]


def gradient_kernel(
    suffix_ref, adjoint_ref, conv_ref, a_ref, i_ref, state_ref, before_ref, branch_ref,
    incoming_ref, entry_ref, taps_ref, table_ref, gate_ref,
    branch_grad_ref, head_ref, sums_ref, gate_grad_ref,
    padded, shifted,
):
    rows, width = conv_ref.shape
    blocks = gate_ref.shape[0]
    block_width = width // blocks
    taps = taps_ref.shape[0]
    step, steps = pl.program_id(0), pl.num_programs(0)

    @pl.when(step == 0)
    def _():
        padded[rows : rows + 8, :] = jnp.zeros((8, width), F32)
        sums_ref[...] = jnp.zeros_like(sums_ref)
        gate_grad_ref[...] = jnp.zeros_like(gate_grad_ref)

    shifted[8 : 8 + rows, :] = state_ref[...]
    shifted[0:8, :] = jnp.where(step == steps - 1, entry_ref[...], before_ref[...])

    def total(values):
        return jnp.sum(values, axis=0, keepdims=True)

    for block in range(blocks):
        columns = slice(block * block_width, (block + 1) * block_width)
        adjoint = adjoint_ref[:, columns] + suffix_ref[:, columns] * incoming_ref[0:1, columns]
        conv, a_rate, i_rate = conv_ref[:, columns], a_ref[:, columns], i_ref[:, columns]
        soft_lambda = table_ref[3:4, columns]
        decay, scale_in = decay_parts(a_rate, soft_lambda)
        before = shifted[7 : 7 + rows, columns]
        weighted = adjoint * i_rate
        grad_log = adjoint * before * decay - weighted * conv * (decay * decay) / scale_in
        rate_part = grad_log * (-DECAY_CONST * a_rate)
        grad_a = rate_part * soft_lambda * (1.0 - a_rate)
        grad_i = weighted * scale_in * conv * (1.0 - i_rate)
        sums_ref[0:1, columns] += total(rate_part)
        sums_ref[1:2, columns] += total(grad_a)
        sums_ref[2:3, columns] += total(grad_i)
        both = jnp.concatenate([grad_a, grad_i], axis=1)
        gate_grad_ref[block] += three_pass(conv, both, ((0,), (0,)))
        back = three_pass(both, gate_ref[block], ((1,), (1,)))
        padded[0:rows, columns] = weighted * scale_in + back
    grad_conv = padded[0:rows, :]
    sums_ref[3:4, :] += total(grad_conv)
    head_ref[...] = grad_conv[0:8, :]
    branch = branch_ref[...]
    branch_grad = jnp.zeros((rows, width), F32)
    for tap in range(taps):
        moved = padded[tap : tap + rows, :]
        branch_grad = branch_grad + taps_ref[tap : tap + 1, :] * moved
        sums_ref[4 + tap : 5 + tap, :] += total(moved * branch)
    branch_grad_ref[...] = branch_grad
    padded[rows : rows + 8, :] = grad_conv[0:8, :]


def block_rows(rows):
    return 256 if rows % 1024 == 0 else rows // 4 if rows % 32 == 0 else rows


def fixed(*shape):
    return pl.BlockSpec(shape, lambda i: (0,) * len(shape))


def shaped(*shape):
    return jax.ShapeDtypeStruct(shape, F32)


def run_forward(branch, edges, taps, table, gates):
    rows, width = branch.shape
    step = block_rows(rows)
    moving = pl.BlockSpec((step, width), lambda i: (i, 0))
    return pl.pallas_call(
        forward_kernel,
        grid=(rows // step,),
        in_specs=[
            moving, fixed(8, width), fixed(*taps.shape), fixed(*table.shape), fixed(*gates.shape)
        ],
        out_specs=[moving] * 5 + [fixed(2, 8, width)],
        out_shape=[shaped(rows, width)] * 5 + [shaped(2, 8, width)],
        scratch_shapes=[pltpu.VMEM((step + 8, width), F32), pltpu.VMEM((2, 8, width), F32)],
        compiler_params=pltpu.CompilerParams(vmem_limit_bytes=VMEM_BYTES),
    )(branch, edges, taps, table, gates)


def run_backward(grad_mixed, gate_pre, rec_state, a_rate, table):
    rows, width = gate_pre.shape
    step = block_rows(rows)
    last, chunks = rows // step - 1, len(grad_mixed)
    each = rows // step // chunks
    moving = pl.BlockSpec((step, width), lambda i: (last - i, 0))

    def of_chunk(place):
        return pl.BlockSpec(
            (step, width), lambda i: (jnp.clip(last - i - place * each, 0, each - 1), 0)
        )

    return pl.pallas_call(
        functools.partial(backward_kernel, chunks=chunks),
        grid=(rows // step,),
        in_specs=[moving] * 3
        + [fixed(*table.shape)]
        + [of_chunk(place) for place in range(chunks)],
        out_specs=[moving] * 3 + [fixed(2, 8, width)],
        out_shape=[shaped(rows, width)] * 3 + [shaped(2, 8, width)],
        scratch_shapes=[pltpu.VMEM((step + 8, width), F32), pltpu.VMEM((2, 8, width), F32)],
        compiler_params=pltpu.CompilerParams(vmem_limit_bytes=VMEM_BYTES),
    )(gate_pre, rec_state, a_rate, table, *grad_mixed)


def run_gradient(
    suffix, adjoint, conv_out, a_rate, i_rate, rec_state, branch, incoming, entry, taps, table, gates
):
    rows, width = branch.shape
    step = block_rows(rows)
    last = rows // step - 1
    moving = pl.BlockSpec((step, width), lambda i: (last - i, 0))
    before = pl.BlockSpec(
        (8, width), lambda i: (jnp.maximum((last - i) * (step // 8) - 1, 0), 0)
    )
    return pl.pallas_call(
        gradient_kernel,
        grid=(rows // step,),
        in_specs=[moving] * 6
        + [before, moving, fixed(8, width), fixed(8, width)]
        + [fixed(*taps.shape), fixed(*table.shape), fixed(*gates.shape)],
        out_specs=[moving, fixed(8, width), fixed(8, width), fixed(*gates.shape)],
        out_shape=[
            shaped(rows, width), shaped(8, width), shaped(8, width), shaped(*gates.shape)
        ],
        scratch_shapes=[pltpu.VMEM((step + 8, width), F32), pltpu.VMEM((step + 8, width), F32)],
        compiler_params=pltpu.CompilerParams(vmem_limit_bytes=VMEM_BYTES),
    )(
        suffix, adjoint, conv_out, a_rate, i_rate, rec_state, rec_state, branch,
        incoming, entry, taps, table, gates,
    )


def product_kernel(span_ref, *refs, count, wide, split):
    left_refs, right_refs = refs[:count], refs[count : count + count * wide]
    outs, (high, low) = refs[count + count * wide : -2], refs[-2:]
    chunk, width = right_refs[0].shape

    @pl.when(pl.program_id(0) == 0)
    def _():
        for place, ref in enumerate(right_refs):
            row, column = place // wide * chunk, place % wide * width
            span = (slice(row, row + chunk), slice(column, column + width))
            high[span], low[span] = halves(ref[...])

    product = None
    for place, ref in enumerate(left_refs):
        span = slice(place * chunk, (place + 1) * chunk)
        left_high, left_low = halves(ref[...])

        def part(one, two):
            return lax.dot_general(
                one, two[span, :], (((0,), (0,)), ((), ())), preferred_element_type=F32
            )

        term = part(left_high, high) + (part(left_high, low) + part(left_low, high))
        product = term if product is None else product + term
    if not split:
        outs[0][...] = product
        return
    rows = product.shape[0] // 2
    first = span_ref[0] == 0
    zero, one = product[:rows], product[rows:]
    outs[0][0] = jnp.where(first, zero, one)
    outs[1][0] = jnp.where(first, one, zero)


def run_product(lefts, rights, wide, split):
    count = len(lefts)
    (chunk, depth), width = lefts[0].shape, rights[0].shape[1]
    shards = lax.axis_size("shard")
    rows = depth // (2 * shards)
    step = 2 * rows if split else 384 if depth % 384 == 0 else depth
    span = lax.axis_index("ctx").astype(jnp.int32).reshape(1)
    if split:
        out_specs = [pl.BlockSpec((1, rows, wide * width), lambda i, span: (i, 0, 0))] * 2
        out_shape = [shaped(shards, rows, wide * width)] * 2
    else:
        out_specs = [pl.BlockSpec((step, wide * width), lambda i, span: (i, 0))]
        out_shape = [shaped(depth, wide * width)]
    return pl.pallas_call(
        functools.partial(product_kernel, count=count, wide=wide, split=split),
        grid_spec=pltpu.PrefetchScalarGridSpec(
            num_scalar_prefetch=1,
            grid=(depth // step,),
            in_specs=[pl.BlockSpec((chunk, step), lambda i, span: (0, i))] * count
            + [
                pl.BlockSpec(
                    (chunk, width), lambda i, span: (0, 0), pipeline_mode=pl.Buffered(1)
                )
            ]
            * (count * wide),
            out_specs=out_specs,
            scratch_shapes=[pltpu.VMEM((count * chunk, wide * width), BF16)] * 2,
        ),
        out_shape=out_shape,
        compiler_params=pltpu.CompilerParams(vmem_limit_bytes=VMEM_BYTES),
    )(span, *lefts, *rights)


def unwritten(rows, width):
    return pl.pallas_call(
        lambda ref: None, out_specs=pl.BlockSpec(memory_space=pl.ANY), out_shape=shaped(rows, width)
    )()


def dot_parts(left_high, left_low, right_high, right_low, dims):
    def part(one, two):
        return lax.dot_general(one, two, (dims, ((), ())), preferred_element_type=F32)

    return part(left_high, right_high) + (part(left_high, right_low) + part(left_low, right_high))


def across_kernel(side_ref, *refs, count):
    lefts, rights = refs[:count], refs[count : 2 * count]
    kept_ref, sent_ref = refs[2 * count : 2 * count + 2]
    scratch = refs[2 * count + 2 :]

    @pl.when(pl.program_id(0) == 0)
    def _():
        for place, ref in enumerate(lefts):
            scratch[2 * place][...], scratch[2 * place + 1][...] = halves(ref[...])

    product = None
    for place in range(count):
        term = dot_parts(
            scratch[2 * place][...], scratch[2 * place + 1][...],
            *halves(rights[place][...]), ((1,), (1,)),
        )
        product = term if product is None else product + term
    half = kept_ref.shape[0]
    first = side_ref[0] == 0
    low, high = product[:half], product[half:]
    kept_ref[...] = jnp.where(first, low, high)
    sent_ref[...] = jnp.where(first, high, low)


def run_across(lefts, rights, columns, chunk, rows):
    count, depth = len(lefts), rights[0].shape[0]
    step = 512 if depth % 512 == 0 else depth
    side = (lax.axis_index("tp") % 2).astype(jnp.int32).reshape(1)
    half = pl.BlockSpec((rows // 2, step), lambda i, side: (0, i))
    widths = [left.shape[1] for left in lefts]
    return pl.pallas_call(
        functools.partial(across_kernel, count=count),
        grid_spec=pltpu.PrefetchScalarGridSpec(
            num_scalar_prefetch=1,
            grid=(depth // step,),
            in_specs=[pl.BlockSpec((rows, w), lambda i, side: (chunk, 0)) for w in widths]
            + [
                pl.BlockSpec((step, w), lambda i, side, column=column: (i, column))
                for w, column in zip(widths, columns)
            ],
            out_specs=[half, half],
            scratch_shapes=[pltpu.VMEM((rows, w), BF16) for w in widths for _ in range(2)],
        ),
        out_shape=[shaped(rows // 2, depth)] * 2,
        compiler_params=pltpu.CompilerParams(vmem_limit_bytes=VMEM_BYTES),
    )(side, *lefts, *rights)


def up_product(value, pre):
    act, slope = gelu_parts(pre)
    return act * value, act, slope * value


def hidden_product(grad_hidden, act, slope_up):
    return grad_hidden * slope_up, grad_hidden * act


def norm_parts(rows):
    inv = lax.rsqrt(jnp.mean(rows * rows, axis=1, keepdims=True) + EPSILON)
    return inv, rows * inv


def norm_back(grad_normed, normed_hat, inv_scale, gain):
    grad_hat = grad_normed * gain
    inner = jnp.mean(grad_hat * normed_hat, axis=1, keepdims=True)
    return (inv_scale * (grad_hat - normed_hat * inner), jnp.sum(grad_normed * normed_hat, axis=0))


def on_device(
    inputs,
    lengths,
    rec_proj,
    gate_proj,
    out_proj,
    ffn_gate,
    ffn_up,
    ffn_down,
    conv_weight,
    conv_bias,
    a_gate,
    i_gate,
    a_bias,
    i_bias,
    lambda_param,
    rec_norm,
    ffn_norm,
    cotangent,
):
    seqs_here, span_len, width_model = inputs.shape
    row_count = seqs_here * span_len
    taps = conv_weight.shape[0]
    width_rec, width_ffn = rec_proj.shape[1], ffn_gate.shape[1]
    chunks = 4
    chunk_rows = row_count // chunks

    def rows_of(values, chunk):
        return values[chunk * chunk_rows : (chunk + 1) * chunk_rows]

    position = lax.axis_index("ctx") * span_len + jnp.arange(span_len, dtype=jnp.int32)
    valid_mask = position[None, :] < lengths[:, None]
    mask_rows = valid_mask.reshape(row_count, 1).astype(F32)

    two_level = lax.axis_size("ctx") == 2
    order = Sequence()
    chunk_list = list(range(chunks))
    scattered = []

    def weight_grad(lefts, rights, wide=1):
        count = len(lefts)
        return order.step(
            lambda *a: run_product(a[:count], a[count:], wide, False)[0], *lefts, *rights
        )

    def split_grad(lefts, rights, wide=1):
        if not two_level:
            return Unsplit(weight_grad(lefts, rights, wide))
        count = len(lefts)
        kept, sent = order.step(
            lambda *a: run_product(a[:count], a[count:], wide, True), *lefts, *rights
        )
        return Scatter(kept, sent, order)

    def scatter(total, axes):
        if scattered:
            order.wait(scattered[-1])
        total = order.gate(total)[0]
        scattered.append(Box(lax.psum_scatter(total, axes, scatter_dimension=0, tiled=True)))
        return scattered[-1]

    everywhere = ("shard", "ctx")

    flat_in = inputs.reshape(row_count, width_model)
    flat_cot = cotangent.reshape(row_count, width_model)
    soft_lambda = jax.nn.softplus(-lambda_param)
    table = jnp.concatenate(
        [jnp.stack([conv_bias, a_bias, i_bias, soft_lambda]), jnp.zeros((4, width_rec), F32)]
    )
    gates = jnp.concatenate([a_gate, i_gate], axis=2)

    def norm_all(rows, gain):
        inv, hat = norm_parts(rows)
        return inv, hat * gain

    blocks = (rec_proj, gate_proj, out_proj, ffn_gate, ffn_up, ffn_down)
    turns = lax.axis_size("shard") - 1
    direct = two_level and turns == 3 and chunks == 4

    def partial(lefts, weights, c, columns=(0, 0)):
        return order.step(
            lambda *a: run_across(a[: len(lefts)], a[len(lefts) :], columns, c, chunk_rows),
            *lefts, *weights,
        )

    def partial_sum(*args):
        return TpSum(*partial(*args), order)

    def gathered(block, *earlier):
        order.wait(*earlier)
        return Box(gather_plain(order.gate(block)[0]))

    fg_weight = Box(gather_plain(ffn_gate))
    pending = []

    def tick(*sends):
        order.wait(*pending)
        pending[:] = [send() for send in sends]

    if direct:
        rec, gbr, out = (Gather(block, order) for block in blocks[:3])
        first = [gbr.swap(), out.swap(), rec.swap()]
        for _ in range(turns):
            tick(rec.turn)
        tick()
        order.wait(first[0], first[1])
        tick(gbr.turn_pair, *([rec.swap] * turns))
        late = pending[1:]
        del pending[1:]
        inv_one, normed_one = order.step(norm_all, flat_in, rec_norm)
        tick(gbr.turn_pair)
        order.wait(*late)
        rec_weight = rec.whole()
    else:
        rec_weight, gbr_weight, out_weight = (Box(gather_plain(block)) for block in blocks[:3])
        inv_one, normed_one = order.step(norm_all, flat_in, rec_norm)
    branch = order.step(matmul, normed_one, rec_weight)
    branch_end = order.step(lambda branch: branch[row_count - (taps - 1) :], branch)
    left_edges = order.send(passed_along, branch_end, "ctx", 1)
    if direct:
        tick(gbr.turn_pair)
        tick(out.turn_pair)
        gbr_weight = gbr.whole()
    gate_pre = order.step(matmul, normed_one, gbr_weight)
    if direct:
        tick(out.turn_pair)
    conv_out, a_rate, i_rate, cumul, local_state, pair = order.step(
        lambda branch, edges, *rest: run_forward(
            branch, jnp.pad(edges, ((8 - (taps - 1), 0), (0, 0))), *rest
        ),
        branch, left_edges, conv_weight, table, gates,
    )
    entry = Box(carried_in(pair.v[0], pair.v[1], 1))
    if direct:
        tick(out.turn_pair)
    fu_weight = gathered(ffn_up, fg_weight)

    def mix(local_state, cumul, entry, gate_pre):
        rec_state = local_state + cumul * entry[0:1]
        return rec_state, rec_state * gelu(gate_pre)

    rec_state, mixed_rows = order.step(mix, local_state, cumul, entry, gate_pre)
    if direct:
        tick()
        out_weight = out.whole()
    mix_sums, after_mix, inv_two, normed_two, gate_in, hidden, acts = (
        [None] * chunks for _ in range(7)
    )

    def start_mix(c):
        mix_sums[c] = partial_sum([mixed_rows], [out_weight], c)

    def take_mix(c):
        def norm_chunk(rows, kept, arriving, gain):
            rows = rows_of(rows, c) + mix_sums[c].rows(kept, arriving)
            inv, hat = norm_parts(rows)
            return rows, inv, hat * gain

        after_mix[c], inv_two[c], normed_two[c] = order.step(
            norm_chunk, flat_in, mix_sums[c].kept, mix_sums[c].arriving, ffn_norm
        )

    def run_gate(c):
        gate_in[c] = order.step(matmul, normed_two[c], fg_weight)

    def run_up(c):
        hidden[c], *acts[c] = order.step(
            lambda left, weight, pre: up_product(matmul(left, weight), pre),
            normed_two[c], fu_weight, gate_in[c],
        )

    grad_result = [None] * chunks

    def mask_chunk(c):
        grad_result[c] = order.step(
            lambda rows, mask: rows_of(rows, c) * rows_of(mask, c), flat_cot, mask_rows
        )

    start_mix(0)
    start_mix(1)
    mix_sums[0].cross()
    start_mix(2)
    mix_sums[1].cross()
    start_mix(3)
    for c in chunk_list:
        mask_chunk(c)
    mix_sums[0].share()
    mix_sums[2].cross()
    take_mix(0)
    run_gate(0)
    mix_sums[1].share()
    mix_sums[3].cross()
    take_mix(1)
    run_gate(1)
    fd_weight = gathered(ffn_down, fu_weight)
    run_up(0)
    mix_sums[2].share()
    run_up(1)
    take_mix(2)
    run_gate(2)
    run_up(2)
    mix_sums[3].share()
    take_mix(3)
    run_gate(3)
    run_up(3)

    ffn_sums, back_sums, grad_pre, grad_up = ([None] * chunks for _ in range(4))
    grad_after_mix, norm_two_sums, grad_mixed = ([None] * chunks for _ in range(3))
    block_out = None

    def start_ffn(c):
        ffn_sums[c] = partial_sum([hidden[c]], [fd_weight], 0)

    def take_ffn(c):
        nonlocal block_out

        def place(rows, kept, arriving, mask, block_out=None):
            rows = (rows + ffn_sums[c].rows(kept, arriving)) * rows_of(mask, c)
            if block_out is None:
                block_out = unwritten(row_count, width_model)
            return lax.dynamic_update_slice(block_out, rows, (c * chunk_rows, 0))

        block_out = order.step(
            place, after_mix[c], ffn_sums[c].kept, ffn_sums[c].arriving, mask_rows,
            *([block_out] if block_out else []),
        )

    def run_hidden(c):
        grad_pre[c], grad_up[c] = order.step(
            lambda left, weight, *acts: hidden_product(matmul(left, weight), *acts),
            grad_result[c], fd_weight, *acts[c],
        )

    def start_back(c):
        back_sums[c] = partial_sum([grad_pre[c], grad_up[c]], [fg_weight, fu_weight], 0)

    def take_back(c):
        def back(rows, after, inv, kept, arriving, gain):
            from_two, norm_sum = norm_back(
                back_sums[c].rows(kept, arriving), after * inv, inv, gain
            )
            return rows + from_two, norm_sum

        grad_after_mix[c], norm_two_sums[c] = order.step(
            back, grad_result[c], after_mix[c], inv_two[c],
            back_sums[c].kept, back_sums[c].arriving, ffn_norm,
        )
        grad_mixed[c] = order.step(matmul, grad_after_mix[c], out_weight)

    rest = chunk_list[2:]
    start_ffn(0)
    start_ffn(1)
    ffn_sums[0].cross()
    ffn_sums[1].cross()
    fd_product = weight_grad(grad_result, hidden)
    grad_fd = scatter(fd_product, everywhere)
    run_hidden(3)
    start_back(3)
    ffn_sums[0].share()
    run_hidden(2)
    back_sums[3].cross()
    take_ffn(0)
    start_back(2)
    ffn_sums[1].share()
    run_hidden(1)
    back_sums[2].cross()
    take_ffn(1)
    start_back(1)
    back_sums[3].share()
    run_hidden(0)
    back_sums[1].cross()
    take_back(3)
    start_back(0)
    back_sums[2].share()
    fg_product = weight_grad(normed_two, grad_pre)
    grad_fg = scatter(fg_product, everywhere)
    back_sums[0].cross()
    take_back(2)
    start_ffn(2)
    back_sums[1].share()
    start_ffn(3)
    ffn_sums[2].cross()
    take_back(1)
    fu_product = weight_grad(normed_two, grad_up)
    ffn_sums[2].share()
    back_sums[0].share()
    ffn_sums[3].cross()
    take_back(0)

    grad_gate_pre, suffix, local_adjoint, back_pair = order.step(
        lambda pre, state, rate, table, *mixed: run_backward(mixed, pre, state, rate, table),
        gate_pre, rec_state, a_rate, table, *grad_mixed,
    )
    ffn_sums[3].share()
    incoming = Box(carried_in(back_pair.v[0], back_pair.v[1], -1))
    order.wait(incoming)
    grad_fu = scatter(fu_product, everywhere)
    grad_branch, head, sums, grad_gates = order.step(
        run_gradient,
        suffix, local_adjoint, conv_out, a_rate, i_rate, rec_state, branch, incoming, entry,
        conv_weight, table, gates,
    )
    head = order.step(lambda head: head[: taps - 1], head)
    right_edges = order.send(passed_along, head, "ctx", -1)

    def tail_rows(grad_branch, right_edges, conv_weight):
        tail = grad_branch[row_count - (taps - 1) :]
        padded_edges = jnp.concatenate([jnp.zeros_like(right_edges), right_edges])
        for tap in range(1, taps):
            tail = tail + conv_weight[tap] * padded_edges[tap : tap + taps - 1]
        return lax.dynamic_update_slice(grad_branch, tail, (row_count - (taps - 1), 0))

    one_sums = [None] * chunks

    def start_one(c):
        one_sums[c] = partial_sum(
            [grad_branch, grad_gate_pre], [rec_weight, gbr_weight], c
        )

    input_grad = None

    def take_one(c):
        nonlocal input_grad

        def back(rows, after, inv, kept, arriving, gain, grads=None):
            inv = rows_of(inv, c)
            from_one, _ = norm_back(
                one_sums[c].rows(kept, arriving), rows_of(after, c) * inv, inv, gain
            )
            if grads is None:
                grads = unwritten(row_count, width_model)
            return lax.dynamic_update_slice(grads, rows + from_one, (c * chunk_rows, 0))

        input_grad = order.step(
            back, grad_after_mix[c], flat_in, inv_one,
            one_sums[c].kept, one_sums[c].arriving, rec_norm,
            *([input_grad] if input_grad else []),
        )

    def small_parts(sums, head, left_edges, grad_gates, lambda_param, *norm_two):
        padded_head = jnp.concatenate([left_edges, jnp.zeros_like(left_edges)])
        edge = taps - 1
        grad_taps = [sums[4]] + [
            sums[4 + tap] + jnp.sum(head * padded_head[edge - tap : 2 * edge - tap], axis=0)
            for tap in range(1, taps)
        ]
        grad_lambda = sums[0] * -jax.nn.sigmoid(-lambda_param)
        vectors = jnp.stack([*grad_taps, sums[1], sums[2], sums[3], grad_lambda])
        return jnp.concatenate(
            [grad_gates.reshape(-1, 128), vectors.reshape(-1, 128), sum(norm_two).reshape(-1, 128)]
        )

    start_one(0)
    start_one(1)
    one_sums[0].cross()
    grad_branch = order.step(tail_rows, grad_branch, right_edges, conv_weight)
    start_one(2)
    one_sums[1].cross()
    start_one(3)
    one_sums[2].cross()
    small = order.step(
        small_parts, sums, head, left_edges, grad_gates, lambda_param, *norm_two_sums
    )
    small = SmallSum(small, order, ("ctx", "shard"))
    small.advance()
    one_sums[3].cross()
    recs = split_grad([normed_one], [grad_branch, grad_gate_pre], wide=2)
    recs.start_ctx()
    outs = split_grad(
        grad_after_mix, order.step(lambda rows: [rows_of(rows, c) for c in chunk_list], mixed_rows)
    )
    outs.start_ctx()
    for c in rest:
        take_ffn(c)
    block_out = block_out.v.reshape(seqs_here, span_len, width_model)

    def gain_sums(gain, rec_weight, gbr_weight, kept, sent=None):
        def rows_sum(grads, which):
            total = 0.0
            for place, weight in enumerate((rec_weight, gbr_weight)):
                if which is not None:
                    weight = weight.reshape(-1, 2, grads.shape[1], width_rec)
                    weight = lax.dynamic_index_in_dim(weight, which, 1, keepdims=False)
                columns = slice(place * width_rec, (place + 1) * width_rec)
                total = total + jnp.sum(grads[..., columns] * weight, axis=-1)
            return total

        if sent is None:
            total = rows_sum(kept, None)
        else:
            span = lax.axis_index("ctx")
            kept, sent = rows_sum(kept, span), rows_sum(sent, 1 - span)
            total = jnp.stack(
                [jnp.where(span == 0, kept, sent), jnp.where(span == 0, sent, kept)], axis=1
            ).reshape(-1)
        return (total / gain).reshape(-1, 128)

    norm_one_sum = order.step(
        gain_sums, rec_norm, rec_weight, gbr_weight, recs.kept,
        *([recs.sent] if two_level else []),
    )
    tiny = SmallSum(norm_one_sum, order, ("tp", "ctx", "shard"))
    order.wait(grad_fu)
    one_sums[0].share()
    one_sums[1].share()
    recs.start_shard()
    one_sums[2].share()
    one_sums[3].share()
    outs.start_shard()
    small.advance()
    grad_recs = recs.result()
    tiny.advance()
    take_one(0)
    tiny.advance()
    take_one(1)
    small.advance()
    tiny.advance()
    take_one(2)
    tiny.advance()
    take_one(3)
    grad_out_proj = outs.result()
    for left in (small, tiny):
        while left.advance():
            pass
    input_grad = input_grad.v.reshape(seqs_here, span_len, width_model)
    small = small.value.v
    sum_norm_one = tiny.value.v.reshape(-1)
    gate_rows = gates.size // 128
    vector_rows = (taps + 4) * width_rec // 128
    sum_gates = small[:gate_rows].reshape(gates.shape)
    vectors = small[gate_rows : gate_rows + vector_rows].reshape(taps + 4, width_rec)
    sum_norm_two = small[gate_rows + vector_rows :].reshape(-1)
    sum_conv_weight = vectors[:taps]
    sum_a_bias, sum_i_bias, sum_conv_bias, sum_lambda = (vectors[taps + k] for k in range(4))
    grad_recs, grad_out_proj, grad_fg, grad_fu, grad_fd = (
        grad.v for grad in (grad_recs, grad_out_proj, grad_fg, grad_fu, grad_fd)
    )
    grad_rec_proj, grad_gate_proj = grad_recs[:, :width_rec], grad_recs[:, width_rec:]
    block_width = a_gate.shape[2]
    return (
        block_out,
        input_grad,
        grad_rec_proj,
        grad_gate_proj,
        grad_out_proj,
        grad_fg,
        grad_fu,
        grad_fd,
        sum_conv_weight,
        sum_conv_bias,
        sum_gates[:, :, :block_width],
        sum_gates[:, :, block_width:],
        sum_a_bias,
        sum_i_bias,
        sum_lambda,
        sum_norm_one,
        sum_norm_two,
    )


def solution(mesh):
    placed = (
        P("shard", "ctx", None),
        P("shard"),
        P(("shard", "ctx"), "tp"),
        P(("shard", "ctx"), "tp"),
        P(("shard", "ctx"), "tp"),
        P(("shard", "ctx"), "tp"),
        P(("shard", "ctx"), "tp"),
        P(("shard", "ctx"), "tp"),
        P(None, "tp"),
        P("tp"),
        P("tp", None, None),
        P("tp", None, None),
        P("tp"),
        P("tp"),
        P("tp"),
        P(),
        P(),
        P("shard", "ctx", None),
    )
    return jax.shard_map(
        on_device,
        mesh=mesh,
        in_specs=placed,
        out_specs=(
            P("shard", "ctx", None),
            P("shard", "ctx", None),
            P(("shard", "ctx"), "tp"),
            P(("shard", "ctx"), "tp"),
            P(("shard", "ctx"), "tp"),
            P(("shard", "ctx"), "tp"),
            P(("shard", "ctx"), "tp"),
            P(("shard", "ctx"), "tp"),
            P(None, "tp"),
            P("tp"),
            P("tp", None, None),
            P("tp", None, None),
            P("tp"),
            P("tp"),
            P("tp"),
            P(),
            P(),
        ),
        check_vma=False,
    )
```
